1024 devices in a mesh: blk: 16 (over x, y_lo, core), dp: 64 (over z, y_hi).
Axes of the slice: x: 4, y: 8 (y_hi: 4, y_lo: 2; y = y_hi * 2 + y_lo), z: 16, core: 2. Of those that a mesh axis runs over, the one named last changes fastest.
Arguments:
- patches: bfloat16 [16, 64, 64, 12, 1152], P('blk', 'dp'), may hold values from -8 to 8
- counts: int32 [16, 64, 64], P('blk'), may hold values from 0 to 12, as said below
- w_qkv: bfloat16 [1152, 1728], replicated, may hold values from -0.1875 to 0.1875
- w_out: bfloat16 [576, 1152], replicated, may hold values from -0.25 to 0.25
- text_rows: bfloat16 [64, 768, 1152], P('dp', 'blk'), may hold values from -160 to 160
- labels: int32 [64, 768], P('dp', 'blk'), may hold values from 0 to 767, each once within a row
Outputs:
- losses: float32 [64, 768], P('dp', 'blk')
- d_pooled: float32 [64, 768, 1152], P('dp', 'blk')
- d_texts: float32 [64, 768, 1152], P('dp', 'blk')
The draws below stay inside these ranges and needn't reach their ends.
Inputs may be any that keep to these rules, and one draw needn't show every extreme that they name: `counts`: A device sends at most one image to each device of its dp group; every device receives exactly 48 images with exactly 384 patches in all, and one of them has exactly 12 patches; a sent image has at least 4 patches. `labels`: each row is a permutation of the group's text indices.
All inputs are finite; a program needn't handle non-finite values.
Results may differ from the reference program's by a relative error of at most 0.0046.
Values may be sent and summed in bfloat16 or wider, within the bound.
A program may use at most 64 MiB of HBM per device.

```python
import jax
import jax.numpy as jnp
from jax import lax

D = 1152
HEADS = 8
HEAD_DIM = 72
CAP = 12
MEAN_PATCH = 8
IMG_DEV = 48
R_DEV = 384
GROUP = 768
N_BLK = 16
N_DP = 64


def draw_counts(key, part):
    key = jax.random.fold_in(key, 11)
    heavy_count = IMG_DEV // 2
    light_count = N_DP - heavy_count
    light_taken = IMG_DEV - heavy_count
    spread_max = CAP - MEAN_PATCH
    pair_count = IMG_DEV // 2

    def one_group(group_key):
        order_key, delta_key, shuffle_key = jax.random.split(group_key, 3)
        source_order = jax.random.permutation(order_key, N_DP).astype(jnp.int32)
        dest_index = jnp.arange(N_DP, dtype=jnp.int32)[:, None]
        slot_index = jnp.arange(IMG_DEV, dtype=jnp.int32)[None, :]
        light_place = heavy_count + (dest_index * light_taken + slot_index - heavy_count) % light_count
        order_place = jnp.where(slot_index < heavy_count, slot_index + 0 * dest_index, light_place)
        source_index = source_order[order_place]
        offsets_drawn = jax.random.randint(delta_key, (N_DP, pair_count), 0, spread_max + 1, dtype=jnp.int32)
        offsets_drawn = offsets_drawn.at[:, 0].set(spread_max)
        row_values = jnp.concatenate([MEAN_PATCH + offsets_drawn, MEAN_PATCH - offsets_drawn], axis=1)
        shuffle_keys = jax.random.split(shuffle_key, N_DP)
        shuffled = jax.vmap(lambda one_key, one_row: jax.random.permutation(one_key, one_row))(shuffle_keys, row_values)
        count_table = jnp.zeros((N_DP, N_DP), jnp.int32)
        return count_table.at[source_index, dest_index + 0 * slot_index].set(shuffled.astype(jnp.int32))
    return jax.vmap(one_group)(jax.random.split(key, N_BLK))


def draw_patches(key, part):
    key = jax.random.fold_in(key, 23)
    row_key, col_key, noise_key = jax.random.split(key, 3)
    full_shape = (N_BLK, N_DP, N_DP, CAP, D)
    row_scale = 10.0 ** jax.random.uniform(row_key, (N_BLK, N_DP, N_DP, CAP, 1), jnp.float32, -1.3, -0.3)
    col_scale = 10.0 ** jax.random.uniform(col_key, (D,), jnp.float32, -0.5, 0.5)
    noise_draw = jnp.clip(jax.random.normal(noise_key, full_shape, jnp.float32), -5.0, 5.0)
    return (noise_draw * row_scale * col_scale).astype(jnp.bfloat16)


def draw_text_rows(key, part):
    key = jax.random.fold_in(key, 37)
    row_key, col_key, noise_key = jax.random.split(key, 3)
    full_shape = (N_DP, N_BLK * IMG_DEV, D)
    row_scale = 10.0 ** jax.random.uniform(row_key, (N_DP, N_BLK * IMG_DEV, 1), jnp.float32, 0.0, 1.0)
    col_scale = 10.0 ** jax.random.uniform(col_key, (D,), jnp.float32, -0.5, 0.5)
    noise_draw = jnp.clip(jax.random.normal(noise_key, full_shape, jnp.float32), -5.0, 5.0)
    return (noise_draw * row_scale * col_scale).astype(jnp.bfloat16)


def gaussian(own_key, dims, deviation, most, held_as=jnp.bfloat16):
    values = deviation * jax.random.normal(own_key, dims, jnp.float32)
    return jnp.clip(values, min=-most, max=most).astype(held_as)


def setup_inputs(seed: int = 0) -> dict:
    seeds = jax.random.split(jax.random.key(seed), 7)
    return {
        "patches": draw_patches(jax.random.fold_in(seeds[6], 71), 0),
        "counts": draw_counts(jax.random.fold_in(seeds[6], 71), 0),
        "w_qkv": gaussian(seeds[2], (D, 3 * HEADS * HEAD_DIM), D ** -0.5, 0.1875),
        "w_out": gaussian(seeds[3], (HEADS * HEAD_DIM, D), (HEADS * HEAD_DIM) ** -0.5, 0.25),
        "text_rows": draw_text_rows(jax.random.fold_in(seeds[6], 71), 0),
        "labels": jax.vmap(lambda own: jax.random.permutation(own, GROUP))(jax.random.split(seeds[5], N_DP)).reshape((N_DP, GROUP)).astype(jnp.int32),
    }


logit_scale = 16.0
logit_bias = -4.0
epsilon = 1e-06

def normalize_rows(values):
    scaling = lax.rsqrt(lax.optimization_barrier(jnp.sum(values * values, axis=-1, keepdims=True)) + epsilon)
    return (values * scaling, scaling)

def attend_images(picked, image_of, w_qkv, w_out):
    widened = picked.astype(jnp.float32)
    centred = widened - lax.optimization_barrier(jnp.mean(widened, axis=-1, keepdims=True))
    spread = lax.optimization_barrier(jnp.mean(centred * centred, axis=-1, keepdims=True))
    normed = (centred * lax.rsqrt(spread + epsilon)).astype(jnp.bfloat16)
    packed = jnp.dot(normed, w_qkv, preferred_element_type=jnp.float32).astype(jnp.bfloat16)
    inner_width = HEADS * HEAD_DIM
    query_rows = packed[:, :inner_width].reshape(R_DEV, HEADS, HEAD_DIM).astype(jnp.float32)
    key_rows = packed[:, inner_width:2 * inner_width].reshape(R_DEV, HEADS, HEAD_DIM).astype(jnp.float32)
    value_rows = packed[:, 2 * inner_width:].reshape(R_DEV, HEADS, HEAD_DIM).astype(jnp.float32)
    scores = jnp.einsum('qhd,khd->hqk', query_rows, key_rows) * HEAD_DIM ** (-0.5)
    same_image = image_of[:, None] == image_of[None, :]
    raised = jnp.where(same_image[None, :, :], jnp.exp(scores), 0.0)
    weights = (raised / lax.optimization_barrier(jnp.sum(raised, axis=-1, keepdims=True))).astype(jnp.bfloat16)
    mixed_heads = jnp.einsum('hqk,khd->qhd', weights.astype(jnp.float32), value_rows)
    mixed_heads = mixed_heads.astype(jnp.bfloat16).reshape(R_DEV, inner_width)
    return widened + jnp.dot(mixed_heads, w_out, preferred_element_type=jnp.float32)

def device_pooled(blocks, intake, w_qkv, w_out):
    sources = intake.shape[0]
    finish = jnp.cumsum(intake)
    starts_at = finish - intake
    living = (intake > 0).astype(jnp.int32)
    ranking = jnp.cumsum(living) - living
    row_ids = jnp.arange(R_DEV, dtype=jnp.int32)
    owning = ((row_ids[:, None] >= starts_at[None, :]) & (row_ids[:, None] < finish[None, :])).astype(jnp.int32)
    source_of = lax.optimization_barrier(jnp.sum(owning * jnp.arange(sources, dtype=jnp.int32)[None, :], axis=1))
    offset_of = lax.optimization_barrier(jnp.sum(owning * starts_at[None, :], axis=1))
    image_of = lax.optimization_barrier(jnp.sum(owning * ranking[None, :], axis=1))
    flat_rows = blocks.reshape(sources * CAP, D)
    picked = jnp.take(flat_rows, (source_of * CAP + row_ids - offset_of).astype(jnp.int32), axis=0)
    result = attend_images(picked, image_of, w_qkv, w_out)
    member = (image_of[None, :] == jnp.arange(IMG_DEV, dtype=jnp.int32)[:, None]).astype(jnp.float32)
    summed = jnp.dot(member, result, precision=lax.Precision.HIGHEST)
    return summed / lax.optimization_barrier(jnp.sum(member, axis=1, keepdims=True))

def group_terms(operands):
    pooled_rows, text_block, label_rows = operands
    unit_img, img_scale = normalize_rows(pooled_rows)
    text_unit, text_scale = normalize_rows(text_block.astype(jnp.float32))
    logits = logit_scale * jnp.dot(unit_img, text_unit.T, precision=lax.Precision.HIGHEST) + logit_bias
    columns = jnp.arange(GROUP, dtype=jnp.int32)
    signed = jnp.where(label_rows[:, None] == columns[None, :], 1.0, -1.0)
    losses = lax.optimization_barrier(jnp.sum(jax.nn.softplus(-signed * logits), axis=1))
    slopes = -signed * jax.nn.sigmoid(-signed * logits)
    grad_img = logit_scale * jnp.dot(slopes, text_unit, precision=lax.Precision.HIGHEST)
    grad_text = logit_scale * jnp.dot(slopes.T, unit_img, precision=lax.Precision.HIGHEST)
    d_pooled = (grad_img - unit_img * lax.optimization_barrier(jnp.sum(unit_img * grad_img, axis=-1, keepdims=True))) * img_scale
    d_texts = (grad_text - text_unit * lax.optimization_barrier(jnp.sum(text_unit * grad_text, axis=-1, keepdims=True))) * text_scale
    return (losses, d_pooled, d_texts)

def reference(patches, counts, w_qkv, w_out, text_rows, labels):
    zero_index = jnp.zeros((), jnp.int32)

    def one_device(flat_index):
        group_index = (flat_index // N_DP).astype(jnp.int32)
        own_place = (flat_index % N_DP).astype(jnp.int32)
        blocks = lax.dynamic_slice(patches, (group_index, zero_index, own_place, zero_index, zero_index), (1, N_DP, 1, CAP, D))
        blocks = blocks.reshape(N_DP, CAP, D)
        intake = lax.dynamic_slice(counts, (group_index, zero_index, own_place), (1, N_DP, 1)).reshape(N_DP)
        return device_pooled(blocks, intake, w_qkv, w_out)
    pooled = lax.map(one_device, jnp.arange(N_BLK * N_DP, dtype=jnp.int32))
    pooled = pooled.reshape(N_BLK, N_DP, IMG_DEV, D).transpose(1, 0, 2, 3).reshape(N_DP, GROUP, D)
    losses, d_pooled, d_texts = lax.map(group_terms, (pooled, text_rows, labels))
    return (losses, d_pooled, d_texts)
```

```python
import functools

import jax
import jax.numpy as jnp
from jax import lax
from jax.experimental import pallas as pl
from jax.experimental.pallas import tpu as pltpu
from jax.sharding import PartitionSpec as P

HEADS = 8
HEAD_DIM = 72
SUBGROUP = 16

logit_scale = 16.0
logit_bias = -4.0
epsilon = 1e-06

NT = (((1,), (1,)), ((), ()))
MESH = pl.DeviceIdType.MESH
STEP_GROUPS = 2
PIECE = 16
LABEL_BASE = 32


def column_of(row):
    n = row.shape[1]
    eye = lax.broadcasted_iota(jnp.int32, (n, n), 0) == lax.broadcasted_iota(jnp.int32, (n, n), 1)
    return jnp.sum(jnp.where(eye, row, jnp.zeros_like(row)), axis=1, keepdims=True)


def row_of(column):
    n = column.shape[0]
    eye = lax.broadcasted_iota(jnp.int32, (n, n), 0) == lax.broadcasted_iota(jnp.int32, (n, n), 1)
    return jnp.sum(jnp.where(eye, column, jnp.zeros_like(column)), axis=0, keepdims=True)


def halves(values):
    high = values.astype(jnp.bfloat16)
    low = (values - high.astype(jnp.float32)).astype(jnp.bfloat16)
    return jnp.concatenate([high, low], axis=0)


def split_dot(values, other):
    rows = values.shape[0]
    both = jnp.dot(halves(values), other, preferred_element_type=jnp.float32)
    return both[:rows] + both[rows:]


def attend_kernel(
    patch_hbm, counts_ref, wt_hbm, wo_hbm, out_ref,
    patch_ref, wt_ref, wo_ref, normed_ref, packed_ref, mean_ref, pool_ref, wide_ref, sent_ref, arrived_ref,
    load_sems, send_sem, recv_sem,
):
    cap, dests, width = patch_ref.shape
    inner = HEADS * HEAD_DIM
    rows = cap * SUBGROUP
    groups = dests // SUBGROUP
    images = out_ref.shape[0]
    half = sent_ref.shape[2]
    me = lax.axis_index("dp")

    loads = [pltpu.make_async_copy(patch_hbm, patch_ref, load_sems.at[0])]
    for p in range(3):
        span = pl.ds(p * inner, inner)
        loads.append(pltpu.make_async_copy(wt_hbm.at[span], wt_ref.at[span], load_sems.at[1 + p]))
    loads.append(pltpu.make_async_copy(wo_hbm, wo_ref, load_sems.at[4]))
    for load in loads:
        load.start()

    barrier = pltpu.get_barrier_semaphore()

    def greet(step, carry):
        pl.semaphore_signal(barrier, inc=1, device_id={"dp": lax.rem(me + step, dests)}, device_id_type=MESH)
        return carry

    lax.fori_loop(1, dests, greet, 0)

    lengths_row = counts_ref[pl.ds(me, 1), :]
    id_row = lax.broadcasted_iota(jnp.int32, (SUBGROUP, dests), 1)
    id_column = lax.broadcasted_iota(jnp.int32, (SUBGROUP, dests), 0)
    order = [lax.rem(lax.div(me, SUBGROUP) + step, groups) for step in (2, 1, 3, 0)[4 - groups :]]
    lengths = [
        jnp.sum(jnp.where(id_row == id_column + g * SUBGROUP, lengths_row, 0), axis=1, keepdims=True) for g in order
    ]
    inverse_lengths = [1.0 / jnp.maximum(length, 1).astype(jnp.float32) for length in lengths]

    loads[0].wait()
    for k, g in enumerate(order):
        total = jnp.zeros((SUBGROUP, width), jnp.float32)
        for r in range(cap):
            block = patch_ref[r, pl.ds(pl.multiple_of(g * SUBGROUP, SUBGROUP), SUBGROUP), :].astype(jnp.float32)
            centred = block - jnp.mean(block, axis=-1, keepdims=True)
            spread = jnp.mean(centred * centred, axis=-1, keepdims=True)
            start = k * rows + r * SUBGROUP
            normed_ref[start : start + SUBGROUP, :] = (centred * lax.rsqrt(spread + epsilon)).astype(jnp.bfloat16)
            total = total + jnp.where(lengths[k] > r, block, 0.0)
        mean_ref[k * SUBGROUP : (k + 1) * SUBGROUP, :] = total * inverse_lengths[k]

    for p in range(3):
        loads[1 + p].wait()
        packed_ref[p] = lax.dot_general(
            normed_ref[...], wt_ref[p * inner : (p + 1) * inner, :], NT, preferred_element_type=jnp.float32
        ).astype(jnp.bfloat16)
    loads[4].wait()

    query_id = lax.broadcasted_iota(jnp.int32, (rows, rows), 0)
    key_id = lax.broadcasted_iota(jnp.int32, (rows, rows), 1)
    same_image = query_id % SUBGROUP == key_id % SUBGROUP
    lane_image = lax.broadcasted_iota(jnp.int32, (SUBGROUP, rows), 1) % SUBGROUP
    pick = lax.broadcasted_iota(jnp.int32, (SUBGROUP, rows), 0) == lane_image
    head_of = lax.broadcasted_iota(jnp.int32, (HEADS, 1, inner), 2)
    head_start = lax.broadcasted_iota(jnp.int32, (HEADS, 1, inner), 0) * HEAD_DIM
    head_mask = ((head_of >= head_start) & (head_of < head_start + HEAD_DIM)).astype(jnp.float32)
    column_id = lax.broadcasted_iota(jnp.int32, (1, inner), 1)

    def pool_group(k):
        key_lengths = jnp.sum(jnp.where(pick, lengths[k], 0), axis=0, keepdims=True)
        query_lengths = jnp.concatenate([lengths[k]] * cap, axis=0)
        query_live = query_id[:, :1] // SUBGROUP < query_lengths
        usable = same_image & (key_id // SUBGROUP < key_lengths) & query_live
        query_share = jnp.concatenate([inverse_lengths[k]] * cap, axis=0)
        group_rows = slice(k * rows, (k + 1) * rows)
        picked = []
        for h in range(HEADS):
            low = h * HEAD_DIM // 128 * 128
            high = min(-(-(h + 1) * HEAD_DIM // 128) * 128, inner)
            window = (column_id[:, low:high] >= h * HEAD_DIM) & (column_id[:, low:high] < (h + 1) * HEAD_DIM)
            queries = packed_ref[0, group_rows, low:high] * window.astype(jnp.bfloat16)
            keys = packed_ref[1, group_rows, low:high]
            scores = lax.dot_general(queries, keys, NT, preferred_element_type=jnp.float32) * HEAD_DIM ** (-0.5)
            raised = jnp.where(usable, jnp.exp(scores), 0.0)
            denominators = jnp.sum(raised, axis=-1, keepdims=True)
            weights = raised * jnp.where(query_live, query_share / denominators, 0.0)
            picked.append(jnp.sum(weights.reshape(cap, SUBGROUP, rows), axis=0))
        stacked = jnp.concatenate(picked, axis=0).astype(jnp.bfloat16)
        mixed = jnp.dot(stacked, packed_ref[2, group_rows, :], preferred_element_type=jnp.float32)
        return jnp.sum(mixed.reshape(HEADS, SUBGROUP, inner) * head_mask, axis=0)

    per_step = STEP_GROUPS
    for first in range(0, groups, per_step):
        members = range(first, min(first + per_step, groups))
        for k in members:
            pool_ref[k * SUBGROUP : (k + 1) * SUBGROUP, :] = pool_group(k)
        span = slice(first * SUBGROUP, (members[-1] + 1) * SUBGROUP)
        result = mean_ref[span, :] + split_dot(pool_ref[span, :], wo_ref[...])
        wide_ref[span, 0, :] = result[:, :half]
        filler = jnp.zeros((result.shape[0], 2 * half - width), jnp.float32)
        wide_ref[span, 1, :] = jnp.concatenate([result[:, half:], filler], axis=1)
        if first == 0:
            pl.semaphore_wait(barrier, dests - 1)
        for k in members:
            base = order[k] * SUBGROUP
            sent_ref[pl.ds(base, SUBGROUP)] = wide_ref[k * SUBGROUP : (k + 1) * SUBGROUP].astype(jnp.bfloat16)

            def send(step, carry, base=base):
                to = base + lax.rem(me + step, SUBGROUP)
                pltpu.make_async_remote_copy(
                    sent_ref.at[to], arrived_ref.at[me], send_sem, recv_sem, device_id={"dp": to}, device_id_type=MESH
                ).start()
                return carry

            lax.fori_loop(1 if k == groups - 1 else 0, SUBGROUP, send, 0)
    arrived_ref[me] = sent_ref[me]

    lane = lax.broadcasted_iota(jnp.int32, (dests, dests), 1)
    sublane = lax.broadcasted_iota(jnp.int32, (dests, dests), 0)
    intake = jnp.sum(jnp.where(lane == me, counts_ref[...], 0), axis=1, keepdims=True)
    living = (intake > 0).astype(jnp.int32)
    living_row = row_of(living)
    ranking_row = jnp.sum(jnp.where(sublane < lane, living, 0), axis=0, keepdims=True)
    image_id = lax.broadcasted_iota(jnp.int32, (images, dests), 0)
    chooser = ((ranking_row == image_id) & (living_row > 0)).astype(jnp.bfloat16)

    pltpu.make_async_remote_copy(
        sent_ref.at[pl.ds(0, dests - 1)], arrived_ref.at[pl.ds(0, dests - 1)], send_sem, recv_sem,
        device_id={"dp": lax.rem(me + 1, dests)}, device_id_type=MESH,
    ).wait()
    wide_ref[...] = arrived_ref[...].astype(jnp.float32)
    for low, high, lane_half in ((0, half, 0), (half, width, 1)):
        values = wide_ref[:, lane_half, : high - low].astype(jnp.bfloat16)
        chosen = jnp.dot(chooser, values, preferred_element_type=jnp.float32)
        out_ref[:, low:high] = chosen.astype(out_ref.dtype)


def attend(patch_rows, count_table, w_qkv_t, w_out, images):
    cap, dests, width = patch_rows.shape
    inner = HEADS * HEAD_DIM
    half = -(-width // 256) * 128
    vmem = pl.BlockSpec(memory_space=pltpu.VMEM)
    hbm = pl.BlockSpec(memory_space=pl.ANY)
    return pl.pallas_call(
        attend_kernel,
        out_shape=jax.ShapeDtypeStruct((images, width), jnp.bfloat16),
        in_specs=[hbm, vmem, hbm, hbm],
        out_specs=vmem,
        scratch_shapes=[
            pltpu.VMEM((cap, dests, width), jnp.bfloat16),
            pltpu.VMEM(w_qkv_t.shape, jnp.bfloat16),
            pltpu.VMEM(w_out.shape, jnp.bfloat16),
            pltpu.VMEM((cap * dests, width), jnp.bfloat16),
            pltpu.VMEM((3, cap * dests, inner), jnp.bfloat16),
            pltpu.VMEM((dests, width), jnp.float32),
            pltpu.VMEM((dests, inner), jnp.float32),
            pltpu.VMEM((dests, 2, half), jnp.float32),
            pltpu.VMEM((dests, 2, half), jnp.bfloat16),
            pltpu.VMEM((dests, 2, half), jnp.bfloat16),
            pltpu.SemaphoreType.DMA((5,)),
            pltpu.SemaphoreType.DMA,
            pltpu.SemaphoreType.DMA,
        ],
        compiler_params=pltpu.CompilerParams(
            collective_id=0, has_side_effects=True, vmem_limit_bytes=56 * 2**20
        ),
        cost_estimate=pl.CostEstimate(flops=5 * 10**9, bytes_accessed=8 * 10**6, transcendentals=10**6),
        name="attend",
    )(patch_rows, count_table, w_qkv_t, w_out)


def inverse_norms(values):
    return lax.rsqrt(jnp.sum(values * values, axis=-1, keepdims=True) + epsilon)


def pair_terms(own, own_scale, others, matching):
    others_scale = row_of(inverse_norms(others.astype(jnp.float32)))
    products = lax.dot_general(own, others, NT, preferred_element_type=jnp.float32)
    logits = logit_scale * (products * own_scale * others_scale) + logit_bias
    sign = jnp.where(matching, 1.0, -1.0)
    margins = -sign * logits
    slopes = -sign / (1.0 + jnp.exp(-margins))
    return margins, slopes * others_scale


def tangent(own, own_scale, gradient):
    unit = own.astype(jnp.float32) * own_scale
    return (gradient - unit * jnp.sum(unit * gradient, axis=-1, keepdims=True)) * own_scale


def contrast_kernel(
    img_ref, payload_hbm, text_ref, label_ref, loss_ref, img_grad_ref, text_grad_ref,
    texts_ref, gathered_ref, load_sem, send_sems, recv_sems,
):
    blocks, images, width = gathered_ref.shape
    me = lax.axis_index("blk")
    sibling = me + 1 - 2 * lax.rem(me, 2)

    def across(block):
        return block + 2 - 4 * lax.rem(lax.div(block, 2), 2)

    def mate(block):
        return block + 1 - 2 * lax.rem(block, 2)

    beside = across(me)
    right, left, opposite = (lax.rem(me + 4 * step, blocks) for step in (1, 3, 2))

    load = pltpu.make_async_copy(payload_hbm, texts_ref, load_sem)
    load.start()
    barrier = pltpu.get_barrier_semaphore()
    for neighbour in (sibling, beside, right, left):
        pl.semaphore_signal(barrier, inc=1, device_id={"blk": neighbour}, device_id_type=MESH)
    gathered_ref[me] = img_ref[...]

    pieces = images // PIECE
    started = []

    def put(stage, c, block, to):
        span = pl.ds(c * PIECE, PIECE)
        place = gathered_ref.at[block, span]
        k = stage * pieces + c
        copy = pltpu.make_async_remote_copy(
            img_ref.at[span] if block is me else place, place, send_sems.at[k], recv_sems.at[k],
            device_id={"blk": to}, device_id_type=MESH,
        )
        copy.start()
        started.append(copy)
        return copy

    own = img_ref[...]
    own_scale = inverse_norms(own.astype(jnp.float32))
    text = text_ref[...]
    text_scale = inverse_norms(text.astype(jnp.float32))
    label_column = column_of(label_ref[...])
    batch = 4
    wide = batch * images
    lane_id = lax.broadcasted_iota(jnp.int32, (images, wide), 1)
    text_id = me * images + lax.broadcasted_iota(jnp.int32, (images, wide), 0)

    def image_batch(q):
        others = texts_ref[batch * q : batch * (q + 1), :images, :].reshape(wide, width)
        margins, weights = pair_terms(own, own_scale, others, label_column == lane_id + q * wide)
        losses = jnp.maximum(margins, 0.0) + jnp.log1p(jnp.exp(-jnp.abs(margins)))
        gradient = split_dot(weights, others)
        if q == 0:
            img_grad_ref[...] = gradient
            return losses
        img_grad_ref[...] += gradient
        return losses

    def text_batch(head, is_first):
        first = lax.div(head, batch) * batch
        others = gathered_ref[pl.ds(first, batch)].reshape(wide, width)
        labels = []
        for i in range(batch):
            tail = texts_ref[first + i, images : images + 16, :images].astype(jnp.float32)
            labels.append(tail[0:1] * LABEL_BASE + tail[1:2])
        matching = jnp.concatenate(labels, axis=1).astype(jnp.int32) == text_id
        _, weights = pair_terms(text, text_scale, others, matching)
        gradient = split_dot(weights, others)
        if is_first:
            text_grad_ref[...] = gradient
        else:
            text_grad_ref[...] += gradient

    each = range(pieces)
    pl.semaphore_wait(barrier, 4)
    to_right = [put(0, c, me, right) for c in each]
    to_left = [put(1, c, me, left) for c in each]
    to_beside = [put(2, c, me, beside) for c in each]
    to_sibling = [put(3, c, me, sibling) for c in each]
    load.wait()
    losses = image_batch(0)

    sibling_waits = []
    beside_right, beside_left, opposite_own = [], [], []
    for c in each:
        to_beside[c].wait_recv()
        beside_right.append(put(4, c, beside, right))
        beside_left.append(put(5, c, beside, left))
        to_right[c].wait_recv()
        to_left[c].wait_recv()
        opposite_own.append(put(6, c, right, left) if c == 1 else put(6, c, left, right))
        sibling_waits.append(put(7, c, beside, sibling))
        sibling_waits.append(put(8, c, left, sibling))
        sibling_waits.append(put(9, c, right, sibling))
        if c + 1 < blocks // batch:
            losses = losses + image_batch(c + 1)
    for q in range(pieces + 1, blocks // batch):
        losses = losses + image_batch(q)

    opposite_beside = []
    for c in each:
        beside_right[c].wait_recv()
        beside_left[c].wait_recv()
        opposite_beside.append(put(10, c, across(left), right) if c == 1 else put(10, c, across(right), left))
        sibling_waits.append(put(11, c, across(left), sibling))
        sibling_waits.append(put(12, c, across(right), sibling))

    for copy in to_sibling:
        copy.wait_recv()
    for copy in sibling_waits[0::3][:pieces]:
        copy.wait_recv()
    text_batch(me, True)
    for c in each:
        opposite_own[c].wait_recv()
        last_own = put(13, c, opposite, sibling)
        opposite_beside[c].wait_recv()
        last_beside = put(14, c, across(opposite), sibling)
        started_last = (last_own, last_beside)
        sibling_waits.extend(started_last)
    for copy in sibling_waits[1 : 3 * pieces : 3] + sibling_waits[2 : 3 * pieces : 3]:
        copy.wait_recv()
    for copy in sibling_waits[3 * pieces : 5 * pieces]:
        copy.wait_recv()
    text_batch(left, False)
    text_batch(right, False)
    loss_ref[...] = row_of(jnp.sum(losses, axis=1, keepdims=True))
    img_grad_ref[...] = tangent(own, own_scale, logit_scale * img_grad_ref[...])
    for copy in sibling_waits[5 * pieces :]:
        copy.wait_recv()
    text_batch(opposite, False)
    text_grad_ref[...] = tangent(text, text_scale, logit_scale * text_grad_ref[...])
    for copy in started:
        copy.wait_send()


def contrast(own_images, payload, own_texts, labels):
    images, width = own_images.shape
    blocks = payload.shape[0]
    copies = 15 * (images // PIECE)
    vmem = pl.BlockSpec(memory_space=pltpu.VMEM)
    hbm = pl.BlockSpec(memory_space=pl.ANY)
    return pl.pallas_call(
        contrast_kernel,
        out_shape=(
            jax.ShapeDtypeStruct((1, images), jnp.float32),
            jax.ShapeDtypeStruct((images, width), jnp.float32),
            jax.ShapeDtypeStruct((images, width), jnp.float32),
        ),
        in_specs=[vmem, hbm, vmem, vmem],
        out_specs=(vmem,) * 3,
        scratch_shapes=[
            pltpu.VMEM(payload.shape, jnp.bfloat16),
            pltpu.VMEM((blocks, images, width), jnp.bfloat16),
            pltpu.SemaphoreType.DMA,
            pltpu.SemaphoreType.DMA((copies,)),
            pltpu.SemaphoreType.DMA((copies,)),
        ],
        compiler_params=pltpu.CompilerParams(
            collective_id=1, has_side_effects=True, vmem_limit_bytes=56 * 2**20
        ),
        cost_estimate=pl.CostEstimate(flops=10**9, bytes_accessed=4 * 10**6, transcendentals=10**5),
        name="contrast",
    )(own_images, payload, own_texts, labels)


def local(patches, counts, w_qkv, w_out, text_rows, labels):
    own_texts = text_rows[0]
    images, width = own_texts.shape
    count_table = counts[0]
    coded = jnp.concatenate([labels // LABEL_BASE, labels % LABEL_BASE], axis=0).astype(jnp.bfloat16)
    tail = jnp.pad(coded, ((0, 16 - coded.shape[0]), (0, width - images)))
    payload = lax.all_gather(jnp.concatenate([own_texts, tail], axis=0), "blk")
    patch_rows = jnp.transpose(patches[0, 0], (1, 0, 2))
    own_images = attend(patch_rows, count_table, w_qkv.T, w_out, images)
    losses, d_pooled, d_texts = contrast(own_images, payload, own_texts, labels)
    return (losses, d_pooled[None], d_texts[None])


def solution(mesh):
    in_specs = (
        P("blk", "dp", None, None, None),
        P("blk", None, None),
        P(),
        P(),
        P("dp", "blk", None),
        P("dp", "blk"),
    )
    out_specs = (P("dp", "blk"), P("dp", "blk", None), P("dp", "blk", None))
    return jax.shard_map(local, mesh=mesh, in_specs=in_specs, out_specs=out_specs, check_vma=False)
```

```python
import functools

import jax
import jax.numpy as jnp
from jax import lax
from jax.experimental import pallas as pl
from jax.experimental.pallas import tpu as pltpu
from jax.sharding import PartitionSpec as P

HEADS = 8
HEAD_DIM = 72
SUBGROUP = 16

logit_scale = 16.0
logit_bias = -4.0
epsilon = 1e-06

NT = (((1,), (1,)), ((), ()))
MESH = pl.DeviceIdType.MESH
STEP_GROUPS = 2
PIECE = 16
LABEL_BASE = 32


def column_of(row):
    n = row.shape[1]
    eye = lax.broadcasted_iota(jnp.int32, (n, n), 0) == lax.broadcasted_iota(jnp.int32, (n, n), 1)
    return jnp.sum(jnp.where(eye, row, jnp.zeros_like(row)), axis=1, keepdims=True)


def row_of(column):
    n = column.shape[0]
    eye = lax.broadcasted_iota(jnp.int32, (n, n), 0) == lax.broadcasted_iota(jnp.int32, (n, n), 1)
    return jnp.sum(jnp.where(eye, column, jnp.zeros_like(column)), axis=0, keepdims=True)


def halves(values):
    high = values.astype(jnp.bfloat16)
    low = (values - high.astype(jnp.float32)).astype(jnp.bfloat16)
    return jnp.concatenate([high, low], axis=0)


def split_dot(values, other):
    rows = values.shape[0]
    both = jnp.dot(halves(values), other, preferred_element_type=jnp.float32)
    return both[:rows] + both[rows:]


def inverse_norms(values):
    return lax.rsqrt(jnp.sum(values * values, axis=-1, keepdims=True) + epsilon)


def pair_terms(own, own_scale, others, others_scale, matching):
    products = lax.dot_general(own, others, NT, preferred_element_type=jnp.float32)
    logits = logit_scale * (products * own_scale * others_scale) + logit_bias
    sign = jnp.where(matching, 1.0, -1.0)
    margins = -sign * logits
    slopes = -sign / (1.0 + jnp.exp(-margins))
    return margins, slopes * others_scale


def tangent(own, own_scale, gradient):
    unit = own.astype(jnp.float32) * own_scale
    return (gradient - unit * jnp.sum(unit * gradient, axis=-1, keepdims=True)) * own_scale


def main_kernel(
    patch_hbm, counts_ref, wt_hbm, wo_hbm, text_ref, label_ref, img_ref, loss_ref, img_grad_ref, text_grad_ref,
    patch_ref, wt_ref, wo_ref, normed_ref, packed_ref, mean_ref, pool_ref, wide_ref, sent_ref, arrived_ref,
    texts_ref, scales_ref, gathered_ref,
    load_sems, send_sem, recv_sem, text_send_sems, text_recv_sems, send_sems, recv_sems,
):
    blocks = texts_ref.shape[0]
    place = lax.axis_index("blk")
    sibling = place + 1 - 2 * lax.rem(place, 2)

    def across(block):
        return block + 2 - 4 * lax.rem(lax.div(block, 2), 2)

    beside = across(place)
    right, left, opposite = (lax.rem(place + 4 * step, blocks) for step in (1, 3, 2))
    peers = (opposite, across(opposite), across(right), across(left), right, left, beside)
    mirror = (0, 1, 3, 2, 5, 4, 6)
    cap, dests, width = patch_ref.shape
    inner = HEADS * HEAD_DIM
    rows = cap * SUBGROUP
    groups = dests // SUBGROUP
    images = img_ref.shape[0]
    half = sent_ref.shape[2]
    me = lax.axis_index("dp")

    loads = [pltpu.make_async_copy(patch_hbm, patch_ref, load_sems.at[0])]
    for p in range(3):
        span = pl.ds(p * inner, inner)
        loads.append(pltpu.make_async_copy(wt_hbm.at[span], wt_ref.at[span], load_sems.at[1 + p]))
    loads.append(pltpu.make_async_copy(wo_hbm, wo_ref, load_sems.at[4]))
    for load in loads:
        load.start()

    barrier = pltpu.get_barrier_semaphore()

    def greet(step, carry):
        pl.semaphore_signal(barrier, inc=1, device_id={"dp": lax.rem(me + step, dests)}, device_id_type=MESH)
        return carry

    lax.fori_loop(1, dests, greet, 0)
    for neighbour in (sibling,) + peers:
        pl.semaphore_signal(barrier, inc=1, device_id={"blk": neighbour}, device_id_type=MESH)

    texts_ref[place, :images, :] = text_ref[...]
    label_row = label_ref[...]
    code_row = lax.broadcasted_iota(jnp.int32, (16, images), 0)
    coded = jnp.where(code_row == 0, label_row // LABEL_BASE, jnp.where(code_row == 1, label_row % LABEL_BASE, 0))
    coded = jnp.concatenate([coded.astype(jnp.float32), jnp.zeros((16, width - images), jnp.float32)], axis=1)
    texts_ref[place, images:, :] = coded.astype(jnp.bfloat16)

    lengths_row = counts_ref[pl.ds(me, 1), :]
    id_row = lax.broadcasted_iota(jnp.int32, (SUBGROUP, dests), 1)
    id_column = lax.broadcasted_iota(jnp.int32, (SUBGROUP, dests), 0)
    order = [lax.rem(lax.div(me, SUBGROUP) + step, groups) for step in (2, 1, 3, 0)[4 - groups :]]
    lengths = [
        jnp.sum(jnp.where(id_row == id_column + g * SUBGROUP, lengths_row, 0), axis=1, keepdims=True) for g in order
    ]
    inverse_lengths = [1.0 / jnp.maximum(length, 1).astype(jnp.float32) for length in lengths]

    loads[0].wait()
    for k, g in enumerate(order):
        total = jnp.zeros((SUBGROUP, width), jnp.float32)
        for r in range(cap):
            block = patch_ref[r, pl.ds(pl.multiple_of(g * SUBGROUP, SUBGROUP), SUBGROUP), :].astype(jnp.float32)
            centred = block - jnp.mean(block, axis=-1, keepdims=True)
            spread = jnp.mean(centred * centred, axis=-1, keepdims=True)
            start = k * rows + r * SUBGROUP
            normed_ref[start : start + SUBGROUP, :] = (centred * lax.rsqrt(spread + epsilon)).astype(jnp.bfloat16)
            total = total + jnp.where(lengths[k] > r, block, 0.0)
        mean_ref[k * SUBGROUP : (k + 1) * SUBGROUP, :] = total * inverse_lengths[k]

    for p in range(3):
        loads[1 + p].wait()
        packed_ref[p] = lax.dot_general(
            normed_ref[...], wt_ref[p * inner : (p + 1) * inner, :], NT, preferred_element_type=jnp.float32
        ).astype(jnp.bfloat16)
    loads[4].wait()

    pl.semaphore_wait(barrier, dests - 1 + 1 + len(peers))

    def pass_text(k, block, to):
        spot = texts_ref.at[block]
        copy = pltpu.make_async_remote_copy(
            spot, spot, text_send_sems.at[k], text_recv_sems.at[k], device_id={"blk": to}, device_id_type=MESH
        )
        copy.start()
        return copy

    text_copies = [pass_text(k, place, to) for k, to in enumerate(peers + (sibling,))]

    query_id = lax.broadcasted_iota(jnp.int32, (rows, rows), 0)
    key_id = lax.broadcasted_iota(jnp.int32, (rows, rows), 1)
    same_image = query_id % SUBGROUP == key_id % SUBGROUP
    lane_image = lax.broadcasted_iota(jnp.int32, (SUBGROUP, rows), 1) % SUBGROUP
    pick = lax.broadcasted_iota(jnp.int32, (SUBGROUP, rows), 0) == lane_image
    head_of = lax.broadcasted_iota(jnp.int32, (HEADS, 1, inner), 2)
    head_start = lax.broadcasted_iota(jnp.int32, (HEADS, 1, inner), 0) * HEAD_DIM
    head_mask = ((head_of >= head_start) & (head_of < head_start + HEAD_DIM)).astype(jnp.float32)
    column_id = lax.broadcasted_iota(jnp.int32, (1, inner), 1)

    def pool_group(k):
        key_lengths = jnp.sum(jnp.where(pick, lengths[k], 0), axis=0, keepdims=True)
        query_lengths = jnp.concatenate([lengths[k]] * cap, axis=0)
        query_live = query_id[:, :1] // SUBGROUP < query_lengths
        usable = same_image & (key_id // SUBGROUP < key_lengths) & query_live
        query_share = jnp.concatenate([inverse_lengths[k]] * cap, axis=0)
        group_rows = slice(k * rows, (k + 1) * rows)
        picked = []
        for h in range(HEADS):
            low = h * HEAD_DIM // 128 * 128
            high = min(-(-(h + 1) * HEAD_DIM // 128) * 128, inner)
            window = (column_id[:, low:high] >= h * HEAD_DIM) & (column_id[:, low:high] < (h + 1) * HEAD_DIM)
            queries = packed_ref[0, group_rows, low:high] * window.astype(jnp.bfloat16)
            keys = packed_ref[1, group_rows, low:high]
            scores = lax.dot_general(queries, keys, NT, preferred_element_type=jnp.float32) * HEAD_DIM ** (-0.5)
            raised = jnp.where(usable, jnp.exp(scores), 0.0)
            denominators = jnp.sum(raised, axis=-1, keepdims=True)
            weights = raised * jnp.where(query_live, query_share / denominators, 0.0)
            picked.append(jnp.sum(weights.reshape(cap, SUBGROUP, rows), axis=0))
        stacked = jnp.concatenate(picked, axis=0).astype(jnp.bfloat16)
        mixed = jnp.dot(stacked, packed_ref[2, group_rows, :], preferred_element_type=jnp.float32)
        return jnp.sum(mixed.reshape(HEADS, SUBGROUP, inner) * head_mask, axis=0)

    per_step = STEP_GROUPS
    for first in range(0, groups, per_step):
        members = range(first, min(first + per_step, groups))
        for k in members:
            pool_ref[k * SUBGROUP : (k + 1) * SUBGROUP, :] = pool_group(k)
        span = slice(first * SUBGROUP, (members[-1] + 1) * SUBGROUP)
        result = mean_ref[span, :] + split_dot(pool_ref[span, :], wo_ref[...])
        wide_ref[span, 0, :] = result[:, :half]
        filler = jnp.zeros((result.shape[0], 2 * half - width), jnp.float32)
        wide_ref[span, 1, :] = jnp.concatenate([result[:, half:], filler], axis=1)
        for k in members:
            base = order[k] * SUBGROUP
            sent_ref[pl.ds(base, SUBGROUP)] = wide_ref[k * SUBGROUP : (k + 1) * SUBGROUP].astype(jnp.bfloat16)

            def send(step, carry, base=base):
                to = base + lax.rem(me + step, SUBGROUP)
                pltpu.make_async_remote_copy(
                    sent_ref.at[to], arrived_ref.at[me], send_sem, recv_sem, device_id={"dp": to}, device_id_type=MESH
                ).start()
                return carry

            lax.fori_loop(1 if k == groups - 1 else 0, SUBGROUP, send, 0)
    arrived_ref[me] = sent_ref[me]

    for k in (6, 4, 5, 2, 3, 0, 1):
        text_copies[k].wait_recv()
        text_copies.append(pass_text(8 + k, peers[mirror[k]], sibling))

    lane = lax.broadcasted_iota(jnp.int32, (dests, dests), 1)
    sublane = lax.broadcasted_iota(jnp.int32, (dests, dests), 0)
    intake = jnp.sum(jnp.where(lane == me, counts_ref[...], 0), axis=1, keepdims=True)
    living = (intake > 0).astype(jnp.int32)
    living_row = row_of(living)
    ranking_row = jnp.sum(jnp.where(sublane < lane, living, 0), axis=0, keepdims=True)
    image_id = lax.broadcasted_iota(jnp.int32, (images, dests), 0)
    chooser = ((ranking_row == image_id) & (living_row > 0)).astype(jnp.bfloat16)

    for copy in text_copies[7:]:
        copy.wait_recv()
    batch = 4
    wide = batch * images

    def text_block(q):
        return texts_ref[batch * q : batch * (q + 1), :images, :].reshape(wide, width)

    for q in range(blocks // batch):
        scales_ref[q : q + 1, :] = row_of(inverse_norms(text_block(q).astype(jnp.float32)))

    pltpu.make_async_remote_copy(
        sent_ref.at[pl.ds(0, dests - 1)], arrived_ref.at[pl.ds(0, dests - 1)], send_sem, recv_sem,
        device_id={"dp": lax.rem(me + 1, dests)}, device_id_type=MESH,
    ).wait()
    wide_ref[...] = arrived_ref[...].astype(jnp.float32)
    for low, high, lane_half in ((0, half, 0), (half, width, 1)):
        values = wide_ref[:, lane_half, : high - low].astype(jnp.bfloat16)
        chosen = jnp.dot(chooser, values, preferred_element_type=jnp.float32)
        img_ref[:, low:high] = chosen.astype(img_ref.dtype)

    gathered_ref[place] = img_ref[...]

    pieces = images // PIECE
    started = []

    def put(stage, c, block, to):
        span = pl.ds(c * PIECE, PIECE)
        spot = gathered_ref.at[block, span]
        k = stage * pieces + c
        copy = pltpu.make_async_remote_copy(
            img_ref.at[span] if block is place else spot, spot, send_sems.at[k], recv_sems.at[k],
            device_id={"blk": to}, device_id_type=MESH,
        )
        copy.start()
        started.append(copy)
        return copy

    own = img_ref[...]
    own_scale = inverse_norms(own.astype(jnp.float32))
    text = text_ref[...]
    text_scale = inverse_norms(text.astype(jnp.float32))
    label_column = column_of(label_ref[...])
    lane_id = lax.broadcasted_iota(jnp.int32, (images, wide), 1)
    text_id = place * images + lax.broadcasted_iota(jnp.int32, (images, wide), 0)

    def image_batch(q):
        others = text_block(q)
        matching = label_column == lane_id + q * wide
        margins, weights = pair_terms(own, own_scale, others, scales_ref[q : q + 1, :], matching)
        losses = jnp.maximum(margins, 0.0) + jnp.log1p(jnp.exp(-jnp.abs(margins)))
        gradient = split_dot(weights, others)
        if q == 0:
            img_grad_ref[...] = gradient
            return losses
        img_grad_ref[...] += gradient
        return losses

    def text_batch(head, is_first):
        first = lax.div(head, batch) * batch
        others = gathered_ref[pl.ds(first, batch)].reshape(wide, width)
        labels = []
        for i in range(batch):
            tail = texts_ref[first + i, images : images + 16, :images].astype(jnp.float32)
            labels.append(tail[0:1] * LABEL_BASE + tail[1:2])
        matching = jnp.concatenate(labels, axis=1).astype(jnp.int32) == text_id
        others_scale = row_of(inverse_norms(others.astype(jnp.float32)))
        _, weights = pair_terms(text, text_scale, others, others_scale, matching)
        gradient = split_dot(weights, others)
        if is_first:
            text_grad_ref[...] = gradient
        else:
            text_grad_ref[...] += gradient

    each = range(pieces)
    to_right = [put(0, c, place, right) for c in each]
    to_left = [put(1, c, place, left) for c in each]
    to_beside = [put(2, c, place, beside) for c in each]
    to_sibling = [put(3, c, place, sibling) for c in each]
    losses = image_batch(0)

    sibling_waits = []
    beside_right, beside_left, opposite_own = [], [], []
    for c in each:
        to_beside[c].wait_recv()
        beside_right.append(put(4, c, beside, right))
        beside_left.append(put(5, c, beside, left))
        to_right[c].wait_recv()
        to_left[c].wait_recv()
        opposite_own.append(put(6, c, right, left) if c == 1 else put(6, c, left, right))
        sibling_waits.append(put(7, c, beside, sibling))
        sibling_waits.append(put(8, c, left, sibling))
        sibling_waits.append(put(9, c, right, sibling))
        if c + 1 < blocks // batch:
            losses = losses + image_batch(c + 1)
    for q in range(pieces + 1, blocks // batch):
        losses = losses + image_batch(q)

    opposite_beside = []
    for c in each:
        beside_right[c].wait_recv()
        beside_left[c].wait_recv()
        opposite_beside.append(put(10, c, across(left), right) if c == 1 else put(10, c, across(right), left))
        sibling_waits.append(put(11, c, across(left), sibling))
        sibling_waits.append(put(12, c, across(right), sibling))

    for copy in to_sibling:
        copy.wait_recv()
    for copy in sibling_waits[0::3][:pieces]:
        copy.wait_recv()
    text_batch(place, True)
    for c in each:
        opposite_own[c].wait_recv()
        last_own = put(13, c, opposite, sibling)
        opposite_beside[c].wait_recv()
        last_beside = put(14, c, across(opposite), sibling)
        started_last = (last_own, last_beside)
        sibling_waits.extend(started_last)
    for copy in sibling_waits[1 : 3 * pieces : 3] + sibling_waits[2 : 3 * pieces : 3]:
        copy.wait_recv()
    for copy in sibling_waits[3 * pieces : 5 * pieces]:
        copy.wait_recv()
    text_batch(left, False)
    text_batch(right, False)
    loss_ref[...] = row_of(jnp.sum(losses, axis=1, keepdims=True))
    for copy in sibling_waits[5 * pieces :]:
        copy.wait_recv()
    text_batch(opposite, False)
    for copy in started + text_copies:
        copy.wait_send()


def main_call(patch_rows, count_table, w_qkv_t, w_out, own_texts, labels, blocks):
    cap, dests, width = patch_rows.shape
    images = own_texts.shape[0]
    inner = HEADS * HEAD_DIM
    half = -(-width // 256) * 128
    copies = 15 * (images // PIECE)
    vmem = pl.BlockSpec(memory_space=pltpu.VMEM)
    hbm = pl.BlockSpec(memory_space=pl.ANY)
    dma = pltpu.SemaphoreType.DMA
    return pl.pallas_call(
        main_kernel,
        out_shape=(
            jax.ShapeDtypeStruct((images, width), jnp.bfloat16),
            jax.ShapeDtypeStruct((1, images), jnp.float32),
            jax.ShapeDtypeStruct((images, width), jnp.float32),
            jax.ShapeDtypeStruct((images, width), jnp.float32),
        ),
        in_specs=[hbm, vmem, hbm, hbm, vmem, vmem],
        out_specs=(vmem,) * 4,
        scratch_shapes=[
            pltpu.VMEM((cap, dests, width), jnp.bfloat16),
            pltpu.VMEM(w_qkv_t.shape, jnp.bfloat16),
            pltpu.VMEM(w_out.shape, jnp.bfloat16),
            pltpu.VMEM((cap * dests, width), jnp.bfloat16),
            pltpu.VMEM((3, cap * dests, inner), jnp.bfloat16),
            pltpu.VMEM((dests, width), jnp.float32),
            pltpu.VMEM((dests, inner), jnp.float32),
            pltpu.VMEM((dests, 2, half), jnp.float32),
            pltpu.VMEM((dests, 2, half), jnp.bfloat16),
            pltpu.VMEM((dests, 2, half), jnp.bfloat16),
            pltpu.VMEM((blocks, images + 16, width), jnp.bfloat16),
            pltpu.VMEM((8, 4 * images), jnp.float32),
            pltpu.VMEM((blocks, images, width), jnp.bfloat16),
            dma((5,)),
            dma,
            dma,
            dma((15,)),
            dma((15,)),
            dma((copies,)),
            dma((copies,)),
        ],
        compiler_params=pltpu.CompilerParams(
            collective_id=0, has_side_effects=True, vmem_limit_bytes=56 * 2**20
        ),
        cost_estimate=pl.CostEstimate(flops=6 * 10**9, bytes_accessed=8 * 10**6, transcendentals=10**6),
        name="main",
    )(patch_rows, count_table, w_qkv_t, w_out, own_texts, labels)


def finish_kernel(img_ref, img_grad_ref, text_ref, text_grad_ref, loss_ref, d_img_ref, d_text_ref, losses_ref):
    for rows_ref, grad_ref, out_ref in ((img_ref, img_grad_ref, d_img_ref), (text_ref, text_grad_ref, d_text_ref)):
        rows = rows_ref[...]
        out_ref[...] = tangent(rows, inverse_norms(rows.astype(jnp.float32)), logit_scale * grad_ref[...])
    losses_ref[...] = loss_ref[...]


def finish(img, img_grad, text, text_grad, losses):
    vmem = pl.BlockSpec(memory_space=pltpu.VMEM)
    return pl.pallas_call(
        finish_kernel,
        out_shape=tuple(jax.ShapeDtypeStruct(v.shape, jnp.float32) for v in (img, text, losses)),
        in_specs=[vmem] * 5,
        out_specs=(vmem,) * 3,
        name="finish",
    )(img, img_grad, text, text_grad, losses)


def local(patches, counts, w_qkv, w_out, text_rows, labels):
    own_texts = text_rows[0]
    patch_rows = jnp.transpose(patches[0, 0], (1, 0, 2))
    img, losses, img_grad, text_grad = main_call(
        patch_rows, counts[0], w_qkv.T, w_out, own_texts, labels, lax.axis_size("blk")
    )
    d_pooled, d_texts, losses = finish(img, img_grad, own_texts, text_grad, losses)
    return (losses, d_pooled[None], d_texts[None])


def solution(mesh):
    in_specs = (
        P("blk", "dp", None, None, None),
        P("blk", None, None),
        P(),
        P(),
        P("dp", "blk", None),
        P("dp", "blk"),
    )
    out_specs = (P("dp", "blk"), P("dp", "blk", None), P("dp", "blk", None))
    return jax.shard_map(local, mesh=mesh, in_specs=in_specs, out_specs=out_specs, check_vma=False)
```

```python
import functools

import jax
import jax.numpy as jnp
from jax import lax
from jax.experimental import pallas as pl
from jax.experimental.pallas import tpu as pltpu
from jax.sharding import PartitionSpec as P

HEADS = 8
HEAD_DIM = 72
SUBGROUP = 16

logit_scale = 16.0
logit_bias = -4.0
epsilon = 1e-06

NT = (((1,), (1,)), ((), ()))
MESH = pl.DeviceIdType.MESH
PIECE = 16


def column_of(row):
    n = row.shape[1]
    eye = lax.broadcasted_iota(jnp.int32, (n, n), 0) == lax.broadcasted_iota(jnp.int32, (n, n), 1)
    return jnp.sum(jnp.where(eye, row, jnp.zeros_like(row)), axis=1, keepdims=True)


def row_of(column):
    n = column.shape[0]
    eye = lax.broadcasted_iota(jnp.int32, (n, n), 0) == lax.broadcasted_iota(jnp.int32, (n, n), 1)
    return jnp.sum(jnp.where(eye, column, jnp.zeros_like(column)), axis=0, keepdims=True)


def halves(values):
    high = values.astype(jnp.bfloat16)
    low = (values - high.astype(jnp.float32)).astype(jnp.bfloat16)
    return jnp.concatenate([high, low], axis=0)


def split_dot(values, other):
    rows = values.shape[0]
    both = jnp.dot(halves(values), other, preferred_element_type=jnp.float32)
    return both[:rows] + both[rows:]


def inverse_norms(values):
    return lax.rsqrt(jnp.sum(values * values, axis=-1, keepdims=True) + epsilon)


def pair_terms(own, own_scale, others, matching):
    others_scale = row_of(inverse_norms(others.astype(jnp.float32)))
    products = lax.dot_general(own, others, NT, preferred_element_type=jnp.float32)
    logits = logit_scale * (products * own_scale * others_scale) + logit_bias
    sign = jnp.where(matching, 1.0, -1.0)
    margins = -sign * logits
    slopes = -sign / (1.0 + jnp.exp(-margins))
    return margins, slopes * others_scale


def tangent(own, own_scale, gradient):
    unit = own.astype(jnp.float32) * own_scale
    return (gradient - unit * jnp.sum(unit * gradient, axis=-1, keepdims=True)) * own_scale


def main_kernel(
    patch_hbm, counts_ref, wt_hbm, wo_hbm, text_ref, label_ref, img_ref, loss_ref, img_grad_ref, text_grad_ref,
    patch_ref, wt_ref, wo_ref, normed_ref, packed_ref, mean_ref, pool_ref, wide_ref, sent_ref, arrived_ref,
    texts_ref, labels_ref, gathered_ref,
    load_sems, send_sem, recv_sem, text_send_sems, text_recv_sems, send_sems, recv_sems,
):
    blocks = texts_ref.shape[0]
    place = lax.axis_index("blk")
    sibling = place + 1 - 2 * lax.rem(place, 2)

    def across(block):
        return block + 2 - 4 * lax.rem(lax.div(block, 2), 2)

    beside = across(place)
    right, left, opposite = (lax.rem(place + 4 * step, blocks) for step in (1, 3, 2))
    peers = (opposite, across(opposite), across(right), across(left), right, left, beside)
    mirror = (0, 1, 3, 2, 5, 4, 6)
    cap, dests, width = patch_ref.shape
    inner = HEADS * HEAD_DIM
    rows = cap * SUBGROUP
    groups = dests // SUBGROUP
    images = img_ref.shape[0]
    half = sent_ref.shape[2]
    me = lax.axis_index("dp")

    loads = [pltpu.make_async_copy(patch_hbm, patch_ref, load_sems.at[0])]
    for p in range(3):
        span = pl.ds(p * inner, inner)
        loads.append(pltpu.make_async_copy(wt_hbm.at[span], wt_ref.at[span], load_sems.at[1 + p]))
    loads.append(pltpu.make_async_copy(wo_hbm, wo_ref, load_sems.at[4]))
    for load in loads:
        load.start()

    barrier = pltpu.get_barrier_semaphore()

    def greet(step, carry):
        pl.semaphore_signal(barrier, inc=1, device_id={"dp": lax.rem(me + step, dests)}, device_id_type=MESH)
        return carry

    lax.fori_loop(1, dests, greet, 0)
    for neighbour in (sibling,) + peers:
        pl.semaphore_signal(barrier, inc=1, device_id={"blk": neighbour}, device_id_type=MESH)

    texts_ref[place] = text_ref[...]
    label_row = jnp.concatenate([label_ref[...], jnp.zeros((1, 128 - images), jnp.int32)], axis=1)
    labels_ref[place] = jnp.broadcast_to(label_row, labels_ref.shape[1:])

    lengths_row = counts_ref[pl.ds(me, 1), :]
    id_row = lax.broadcasted_iota(jnp.int32, (SUBGROUP, dests), 1)
    id_column = lax.broadcasted_iota(jnp.int32, (SUBGROUP, dests), 0)
    order = [lax.rem(lax.div(me, SUBGROUP) + step, groups) for step in (2, 1, 3, 0)[4 - groups :]]
    lengths = [
        jnp.sum(jnp.where(id_row == id_column + g * SUBGROUP, lengths_row, 0), axis=1, keepdims=True) for g in order
    ]
    inverse_lengths = [1.0 / jnp.maximum(length, 1).astype(jnp.float32) for length in lengths]

    loads[0].wait()
    for k, g in enumerate(order):
        total = jnp.zeros((SUBGROUP, width), jnp.float32)
        for r in range(cap):
            block = patch_ref[r, pl.ds(pl.multiple_of(g * SUBGROUP, SUBGROUP), SUBGROUP), :].astype(jnp.float32)
            centred = block - jnp.mean(block, axis=-1, keepdims=True)
            spread = jnp.mean(centred * centred, axis=-1, keepdims=True)
            start = k * rows + r * SUBGROUP
            normed_ref[start : start + SUBGROUP, :] = (centred * lax.rsqrt(spread + epsilon)).astype(jnp.bfloat16)
            total = total + jnp.where(lengths[k] > r, block, 0.0)
        mean_ref[k * SUBGROUP : (k + 1) * SUBGROUP, :] = total * inverse_lengths[k]

    for p in range(3):
        loads[1 + p].wait()
        packed_ref[p] = lax.dot_general(
            normed_ref[...], wt_ref[p * inner : (p + 1) * inner, :], NT, preferred_element_type=jnp.float32
        ).astype(jnp.bfloat16)
    loads[4].wait()

    query_id = lax.broadcasted_iota(jnp.int32, (rows, rows), 0)
    key_id = lax.broadcasted_iota(jnp.int32, (rows, rows), 1)
    same_image = query_id % SUBGROUP == key_id % SUBGROUP
    lane_image = lax.broadcasted_iota(jnp.int32, (SUBGROUP, rows), 1) % SUBGROUP
    pick = lax.broadcasted_iota(jnp.int32, (SUBGROUP, rows), 0) == lane_image
    head_of = lax.broadcasted_iota(jnp.int32, (HEADS, 1, inner), 2)
    head_start = lax.broadcasted_iota(jnp.int32, (HEADS, 1, inner), 0) * HEAD_DIM
    head_mask = ((head_of >= head_start) & (head_of < head_start + HEAD_DIM)).astype(jnp.float32)
    column_id = lax.broadcasted_iota(jnp.int32, (1, inner), 1)
    ones = jnp.ones((rows, 128), jnp.bfloat16)
    largest = float(jnp.finfo(jnp.bfloat16).max)

    def pool_group(k):
        key_lengths = jnp.sum(jnp.where(pick, lengths[k], 0), axis=0, keepdims=True)
        query_lengths = jnp.concatenate([lengths[k]] * cap, axis=0)
        query_live = query_id[:, :1] // SUBGROUP < query_lengths
        usable = same_image & (key_id // SUBGROUP < key_lengths) & query_live
        query_share = jnp.concatenate([inverse_lengths[k]] * cap, axis=0)
        group_rows = slice(k * rows, (k + 1) * rows)
        picked = []
        for h in range(HEADS):
            low = h * HEAD_DIM // 128 * 128
            high = min(-(-(h + 1) * HEAD_DIM // 128) * 128, inner)
            window = (column_id[:, low:high] >= h * HEAD_DIM) & (column_id[:, low:high] < (h + 1) * HEAD_DIM)
            queries = packed_ref[0, group_rows, low:high] * window.astype(jnp.bfloat16)
            keys = packed_ref[1, group_rows, low:high]
            scores = lax.dot_general(queries, keys, NT, preferred_element_type=jnp.float32) * HEAD_DIM ** (-0.5)
            raised = jnp.where(usable, jnp.minimum(jnp.exp(scores), largest), 0.0).astype(jnp.bfloat16)
            denominators = jnp.dot(raised, ones, preferred_element_type=jnp.float32)
            share = jnp.where(query_live, query_share / denominators, 0.0)
            share = jnp.concatenate([share, share[:, : rows - 128]], axis=1)
            weights = raised.astype(jnp.float32) * share
            picked.append(jnp.sum(weights.reshape(cap, SUBGROUP, rows), axis=0))
        stacked = jnp.concatenate(picked, axis=0).astype(jnp.bfloat16)
        mixed = jnp.dot(stacked, packed_ref[2, group_rows, :], preferred_element_type=jnp.float32)
        return jnp.sum(mixed.reshape(HEADS, SUBGROUP, inner) * head_mask, axis=0)

    text_copies, label_copies = [], []

    def pass_text(k, block, to):
        for ref, sems, copies in ((texts_ref, 0, text_copies), (labels_ref, 15, label_copies)):
            spot = ref.at[block]
            copy = pltpu.make_async_remote_copy(
                spot, spot, text_send_sems.at[sems + k], text_recv_sems.at[sems + k],
                device_id={"blk": to}, device_id_type=MESH,
            )
            copy.start()
            copies.append(copy)

    for members in (range(groups - 1), range(groups - 1, groups)):
        for k in members:
            pool_ref[k * SUBGROUP : (k + 1) * SUBGROUP, :] = pool_group(k)
        span = slice(members[0] * SUBGROUP, (members[-1] + 1) * SUBGROUP)
        result = mean_ref[span, :] + split_dot(pool_ref[span, :], wo_ref[...])
        wide_ref[span, 0, :] = result[:, :half]
        filler = jnp.zeros((result.shape[0], 2 * half - width), jnp.float32)
        wide_ref[span, 1, :] = jnp.concatenate([result[:, half:], filler], axis=1)
        if members[0] == 0:
            pl.semaphore_wait(barrier, dests - 1 + 1 + len(peers))
        for k in members:
            base = order[k] * SUBGROUP
            sent_ref[pl.ds(base, SUBGROUP)] = wide_ref[k * SUBGROUP : (k + 1) * SUBGROUP].astype(jnp.bfloat16)

            def send(step, carry, base=base):
                to = base + lax.rem(me + step, SUBGROUP)
                pltpu.make_async_remote_copy(
                    sent_ref.at[to], arrived_ref.at[me], send_sem, recv_sem, device_id={"dp": to}, device_id_type=MESH
                ).start()
                return carry

            lax.fori_loop(1 if k == groups - 1 else 0, SUBGROUP, send, 0)
        if members[0] == 0:
            for k, to in enumerate(peers + (sibling,)):
                pass_text(k, place, to)
    arrived_ref[me] = sent_ref[me]

    lane = lax.broadcasted_iota(jnp.int32, (dests, dests), 1)
    sublane = lax.broadcasted_iota(jnp.int32, (dests, dests), 0)
    intake = jnp.sum(jnp.where(lane == me, counts_ref[...], 0), axis=1, keepdims=True)
    living = (intake > 0).astype(jnp.int32)
    living_row = row_of(living)
    ranking_row = jnp.sum(jnp.where(sublane < lane, living, 0), axis=0, keepdims=True)
    image_id = lax.broadcasted_iota(jnp.int32, (images, dests), 0)
    chooser = ((ranking_row == image_id) & (living_row > 0)).astype(jnp.bfloat16)

    batch = 4
    wide = batch * images

    pltpu.make_async_remote_copy(
        sent_ref.at[pl.ds(0, dests - 1)], arrived_ref.at[pl.ds(0, dests - 1)], send_sem, recv_sem,
        device_id={"dp": lax.rem(me + 1, dests)}, device_id_type=MESH,
    ).wait()
    wide_ref[...] = arrived_ref[...].astype(jnp.float32)
    for low, high, lane_half in ((0, half, 0), (half, width, 1)):
        values = wide_ref[:, lane_half, : high - low].astype(jnp.bfloat16)
        chosen = jnp.dot(chooser, values, preferred_element_type=jnp.float32)
        img_ref[:, low:high] = chosen.astype(img_ref.dtype)

    gathered_ref[place] = img_ref[...]

    pieces = images // PIECE
    started = []

    def put(stage, c, block, to):
        span = pl.ds(c * PIECE, PIECE)
        spot = gathered_ref.at[block, span]
        k = stage * pieces + c
        copy = pltpu.make_async_remote_copy(
            img_ref.at[span] if block is place else spot, spot, send_sems.at[k], recv_sems.at[k],
            device_id={"blk": to}, device_id_type=MESH,
        )
        copy.start()
        started.append(copy)
        return copy

    own = img_ref[...]
    own_scale = inverse_norms(own.astype(jnp.float32))
    text = text_ref[...]
    text_scale = inverse_norms(text.astype(jnp.float32))
    label_column = column_of(label_ref[...])
    lane_id = lax.broadcasted_iota(jnp.int32, (images, wide), 1)
    text_id = place * images + lax.broadcasted_iota(jnp.int32, (images, wide), 0)

    def image_batch(q):
        others = texts_ref[batch * q : batch * (q + 1)].reshape(wide, width)
        matching = label_column == lane_id + q * wide
        margins, weights = pair_terms(own, own_scale, others, matching)
        losses = jnp.maximum(margins, 0.0) + jnp.log1p(jnp.exp(-jnp.abs(margins)))
        gradient = split_dot(weights, others)
        if q == 0:
            img_grad_ref[...] = gradient
            return losses
        img_grad_ref[...] += gradient
        return losses

    def text_batch(head, is_first):
        first = lax.div(head, batch) * batch
        others = gathered_ref[pl.ds(first, batch)].reshape(wide, width)
        labels = [labels_ref[first + i, 0:1, :images] for i in range(batch)]
        matching = jnp.concatenate(labels, axis=1) == text_id
        _, weights = pair_terms(text, text_scale, others, matching)
        gradient = split_dot(weights, others)
        if is_first:
            text_grad_ref[...] = gradient
        else:
            text_grad_ref[...] += gradient

    each = range(pieces)
    to_right = [put(0, c, place, right) for c in each]
    to_left = [put(1, c, place, left) for c in each]
    to_beside = [put(2, c, place, beside) for c in each]
    to_sibling = [put(3, c, place, sibling) for c in each]
    for k in (6, 4, 5, 2, 3, 0, 1):
        text_copies[k].wait_recv()
        label_copies[k].wait_recv()
        pass_text(8 + k, peers[mirror[k]], sibling)

    sibling_waits = []
    beside_right, beside_left, opposite_own = [], [], []
    for c in each:
        to_beside[c].wait_recv()
        beside_right.append(put(4, c, beside, right))
        beside_left.append(put(5, c, beside, left))
        to_right[c].wait_recv()
        to_left[c].wait_recv()
        opposite_own.append(put(6, c, right, left) if c == 1 else put(6, c, left, right))
        sibling_waits.append(put(7, c, beside, sibling))
        sibling_waits.append(put(8, c, left, sibling))
        sibling_waits.append(put(9, c, right, sibling))

    for copy in text_copies[7:] + label_copies[7:]:
        copy.wait_recv()
    losses = image_batch(0)
    opposite_beside = []
    for c in each:
        beside_right[c].wait_recv()
        beside_left[c].wait_recv()
        opposite_beside.append(put(10, c, across(left), right) if c == 1 else put(10, c, across(right), left))
        sibling_waits.append(put(11, c, across(left), sibling))
        sibling_waits.append(put(12, c, across(right), sibling))
        if c + 1 < blocks // batch:
            losses = losses + image_batch(c + 1)
    for q in range(pieces + 1, blocks // batch):
        losses = losses + image_batch(q)

    for copy in to_sibling:
        copy.wait_recv()
    for copy in sibling_waits[0::3][:pieces]:
        copy.wait_recv()
    text_batch(place, True)
    for c in each:
        opposite_own[c].wait_recv()
        last_own = put(13, c, opposite, sibling)
        opposite_beside[c].wait_recv()
        last_beside = put(14, c, across(opposite), sibling)
        started_last = (last_own, last_beside)
        sibling_waits.extend(started_last)
    for copy in sibling_waits[1 : 3 * pieces : 3] + sibling_waits[2 : 3 * pieces : 3]:
        copy.wait_recv()
    for copy in sibling_waits[3 * pieces : 5 * pieces]:
        copy.wait_recv()
    text_batch(left, False)
    text_batch(right, False)
    loss_ref[...] = row_of(jnp.sum(losses, axis=1, keepdims=True))
    for copy in sibling_waits[5 * pieces :]:
        copy.wait_recv()
    text_batch(opposite, False)
    for copy in started + text_copies + label_copies:
        copy.wait_send()


def main_call(patch_rows, count_table, w_qkv_t, w_out, own_texts, labels, blocks):
    cap, dests, width = patch_rows.shape
    images = own_texts.shape[0]
    inner = HEADS * HEAD_DIM
    half = -(-width // 256) * 128
    copies = 15 * (images // PIECE)
    vmem = pl.BlockSpec(memory_space=pltpu.VMEM)
    hbm = pl.BlockSpec(memory_space=pl.ANY)
    dma = pltpu.SemaphoreType.DMA
    return pl.pallas_call(
        main_kernel,
        out_shape=(
            jax.ShapeDtypeStruct((images, width), jnp.bfloat16),
            jax.ShapeDtypeStruct((1, images), jnp.float32),
            jax.ShapeDtypeStruct((images, width), jnp.float32),
            jax.ShapeDtypeStruct((images, width), jnp.float32),
        ),
        in_specs=[hbm, vmem, hbm, hbm, vmem, vmem],
        out_specs=(vmem,) * 4,
        scratch_shapes=[
            pltpu.VMEM((cap, dests, width), jnp.bfloat16),
            pltpu.VMEM(w_qkv_t.shape, jnp.bfloat16),
            pltpu.VMEM(w_out.shape, jnp.bfloat16),
            pltpu.VMEM((cap * dests, width), jnp.bfloat16),
            pltpu.VMEM((3, cap * dests, inner), jnp.bfloat16),
            pltpu.VMEM((dests, width), jnp.float32),
            pltpu.VMEM((dests, inner), jnp.float32),
            pltpu.VMEM((dests, 2, half), jnp.float32),
            pltpu.VMEM((dests, 2, half), jnp.bfloat16),
            pltpu.VMEM((dests, 2, half), jnp.bfloat16),
            pltpu.VMEM((blocks, images, width), jnp.bfloat16),
            pltpu.VMEM((blocks, 8, 128), jnp.int32),
            pltpu.VMEM((blocks, images, width), jnp.bfloat16),
            dma((5,)),
            dma,
            dma,
            dma((30,)),
            dma((30,)),
            dma((copies,)),
            dma((copies,)),
        ],
        compiler_params=pltpu.CompilerParams(
            collective_id=0, has_side_effects=True, vmem_limit_bytes=56 * 2**20
        ),
        cost_estimate=pl.CostEstimate(flops=6 * 10**9, bytes_accessed=8 * 10**6, transcendentals=10**6),
        name="main",
    )(patch_rows, count_table, w_qkv_t, w_out, own_texts, labels)


def finish_kernel(img_ref, img_grad_ref, text_ref, text_grad_ref, loss_ref, d_img_ref, d_text_ref, losses_ref):
    for rows_ref, grad_ref, out_ref in ((img_ref, img_grad_ref, d_img_ref), (text_ref, text_grad_ref, d_text_ref)):
        rows = rows_ref[...]
        out_ref[...] = tangent(rows, inverse_norms(rows.astype(jnp.float32)), logit_scale * grad_ref[...])
    losses_ref[...] = loss_ref[...]


def finish(img, img_grad, text, text_grad, losses):
    vmem = pl.BlockSpec(memory_space=pltpu.VMEM)
    return pl.pallas_call(
        finish_kernel,
        out_shape=tuple(jax.ShapeDtypeStruct(v.shape, jnp.float32) for v in (img, text, losses)),
        in_specs=[vmem] * 5,
        out_specs=(vmem,) * 3,
        name="finish",
    )(img, img_grad, text, text_grad, losses)


def local(patches, counts, w_qkv, w_out, text_rows, labels):
    own_texts = text_rows[0]
    patch_rows = jnp.transpose(patches[0, 0], (1, 0, 2))
    img, losses, img_grad, text_grad = main_call(
        patch_rows, counts[0], w_qkv.T, w_out, own_texts, labels, lax.axis_size("blk")
    )
    d_pooled, d_texts, losses = finish(img, img_grad, own_texts, text_grad, losses)
    return (losses, d_pooled[None], d_texts[None])


def solution(mesh):
    in_specs = (
        P("blk", "dp", None, None, None),
        P("blk", None, None),
        P(),
        P(),
        P("dp", "blk", None),
        P("dp", "blk"),
    )
    out_specs = (P("dp", "blk"), P("dp", "blk", None), P("dp", "blk", None))
    return jax.shard_map(local, mesh=mesh, in_specs=in_specs, out_specs=out_specs, check_vma=False)
```

```python
import functools

import jax
import jax.numpy as jnp
from jax import lax
from jax.experimental import pallas as pl
from jax.experimental.pallas import tpu as pltpu
from jax.sharding import PartitionSpec as P

HEADS = 8
HEAD_DIM = 72
SUBGROUP = 16

logit_scale = 16.0
logit_bias = -4.0
epsilon = 1e-06

NT = (((1,), (1,)), ((), ()))
MESH = pl.DeviceIdType.MESH
PIECE = 16


def column_of(row):
    n = row.shape[1]
    eye = lax.broadcasted_iota(jnp.int32, (n, n), 0) == lax.broadcasted_iota(jnp.int32, (n, n), 1)
    return jnp.sum(jnp.where(eye, row, jnp.zeros_like(row)), axis=1, keepdims=True)


def row_of(column):
    n = column.shape[0]
    eye = lax.broadcasted_iota(jnp.int32, (n, n), 0) == lax.broadcasted_iota(jnp.int32, (n, n), 1)
    return jnp.sum(jnp.where(eye, column, jnp.zeros_like(column)), axis=0, keepdims=True)


def halves(values):
    high = values.astype(jnp.bfloat16)
    low = (values - high.astype(jnp.float32)).astype(jnp.bfloat16)
    return jnp.concatenate([high, low], axis=0)


def split_dot(values, other):
    rows = values.shape[0]
    both = jnp.dot(halves(values), other, preferred_element_type=jnp.float32)
    return both[:rows] + both[rows:]


def inverse_norms(values):
    return lax.rsqrt(jnp.sum(values * values, axis=-1, keepdims=True) + epsilon)


def pair_terms(own, own_scale, others, matching):
    others_scale = row_of(inverse_norms(others.astype(jnp.float32)))
    products = lax.dot_general(own, others, NT, preferred_element_type=jnp.float32)
    logits = logit_scale * (products * own_scale * others_scale) + logit_bias
    sign = jnp.where(matching, 1.0, -1.0)
    margins = -sign * logits
    slopes = -sign / (1.0 + jnp.exp(-margins))
    return margins, slopes * others_scale


def tangent(own, own_scale, gradient):
    unit = own.astype(jnp.float32) * own_scale
    return (gradient - unit * jnp.sum(unit * gradient, axis=-1, keepdims=True)) * own_scale


def main_kernel(
    patch_hbm, counts_ref, wt_hbm, wo_hbm, text_ref, label_ref, img_ref, loss_ref, img_grad_ref, text_grad_ref,
    patch_ref, wt_ref, wo_ref, normed_ref, packed_ref, mean_ref, pool_ref, wide_ref, sent_ref, arrived_ref,
    texts_ref, labels_ref, gathered_ref,
    load_sems, send_sem, recv_sem, text_send_sems, text_recv_sems, send_sems, recv_sems,
):
    blocks = texts_ref.shape[0]
    place = lax.axis_index("blk")
    sibling = place + 1 - 2 * lax.rem(place, 2)

    def across(block):
        return block + 2 - 4 * lax.rem(lax.div(block, 2), 2)

    beside = across(place)
    right, left, opposite = (lax.rem(place + 4 * step, blocks) for step in (1, 3, 2))
    targets = (across(right), across(left), right, left, beside, sibling)
    sources = (across(left), across(right), left, right, beside, sibling)
    cap, dests, width = patch_ref.shape
    inner = HEADS * HEAD_DIM
    rows = cap * SUBGROUP
    groups = dests // SUBGROUP
    images = img_ref.shape[0]
    half = sent_ref.shape[2]
    me = lax.axis_index("dp")

    loads = [pltpu.make_async_copy(patch_hbm, patch_ref, load_sems.at[0])]
    for p in range(3):
        span = pl.ds(p * inner, inner)
        loads.append(pltpu.make_async_copy(wt_hbm.at[span], wt_ref.at[span], load_sems.at[1 + p]))
    loads.append(pltpu.make_async_copy(wo_hbm, wo_ref, load_sems.at[4]))
    for load in loads:
        load.start()

    barrier = pltpu.get_barrier_semaphore()

    def greet(step, carry):
        pl.semaphore_signal(barrier, inc=1, device_id={"dp": lax.rem(me + step, dests)}, device_id_type=MESH)
        return carry

    lax.fori_loop(1, dests, greet, 0)
    for neighbour in targets:
        pl.semaphore_signal(barrier, inc=1, device_id={"blk": neighbour}, device_id_type=MESH)

    texts_ref[place] = text_ref[...]
    label_row = jnp.concatenate([label_ref[...], jnp.zeros((1, 128 - images), jnp.int32)], axis=1)
    labels_ref[place] = jnp.broadcast_to(label_row, labels_ref.shape[1:])

    lengths_row = counts_ref[pl.ds(me, 1), :]
    id_row = lax.broadcasted_iota(jnp.int32, (SUBGROUP, dests), 1)
    id_column = lax.broadcasted_iota(jnp.int32, (SUBGROUP, dests), 0)
    order = [lax.rem(lax.div(me, SUBGROUP) + step, groups) for step in (2, 1, 3, 0)[4 - groups :]]
    lengths = [
        jnp.sum(jnp.where(id_row == id_column + g * SUBGROUP, lengths_row, 0), axis=1, keepdims=True) for g in order
    ]
    inverse_lengths = [1.0 / jnp.maximum(length, 1).astype(jnp.float32) for length in lengths]

    loads[0].wait()
    for k, g in enumerate(order):
        total = jnp.zeros((SUBGROUP, width), jnp.float32)
        for r in range(cap):
            block = patch_ref[r, pl.ds(pl.multiple_of(g * SUBGROUP, SUBGROUP), SUBGROUP), :].astype(jnp.float32)
            centred = block - jnp.mean(block, axis=-1, keepdims=True)
            spread = jnp.mean(centred * centred, axis=-1, keepdims=True)
            start = k * rows + r * SUBGROUP
            normed_ref[start : start + SUBGROUP, :] = (centred * lax.rsqrt(spread + epsilon)).astype(jnp.bfloat16)
            total = total + jnp.where(lengths[k] > r, block, 0.0)
        mean_ref[k * SUBGROUP : (k + 1) * SUBGROUP, :] = total * inverse_lengths[k]

    for p in range(3):
        loads[1 + p].wait()
        packed_ref[p] = lax.dot_general(
            normed_ref[...], wt_ref[p * inner : (p + 1) * inner, :], NT, preferred_element_type=jnp.float32
        ).astype(jnp.bfloat16)
    loads[4].wait()

    pl.semaphore_wait(barrier, dests - 1 + len(targets))
    text_copies, label_copies = [], []

    def pass_text(k, block, to):
        for ref, sems, copies in ((texts_ref, 0, text_copies), (labels_ref, 15, label_copies)):
            spot = ref.at[block]
            copy = pltpu.make_async_remote_copy(
                spot, spot, text_send_sems.at[sems + k], text_recv_sems.at[sems + k],
                device_id={"blk": to}, device_id_type=MESH,
            )
            copy.start()
            copies.append(copy)

    for k, to in enumerate(targets):
        pass_text(k, place, to)

    query_id = lax.broadcasted_iota(jnp.int32, (rows, rows), 0)
    key_id = lax.broadcasted_iota(jnp.int32, (rows, rows), 1)
    same_image = query_id % SUBGROUP == key_id % SUBGROUP
    lane_image = lax.broadcasted_iota(jnp.int32, (SUBGROUP, rows), 1) % SUBGROUP
    pick = lax.broadcasted_iota(jnp.int32, (SUBGROUP, rows), 0) == lane_image
    head_of = lax.broadcasted_iota(jnp.int32, (HEADS, 1, inner), 2)
    head_start = lax.broadcasted_iota(jnp.int32, (HEADS, 1, inner), 0) * HEAD_DIM
    head_mask = ((head_of >= head_start) & (head_of < head_start + HEAD_DIM)).astype(jnp.float32)
    column_id = lax.broadcasted_iota(jnp.int32, (1, inner), 1)
    ones = jnp.ones((rows, 128), jnp.bfloat16)
    largest = float(jnp.finfo(jnp.bfloat16).max)

    def pool_group(k):
        key_lengths = jnp.sum(jnp.where(pick, lengths[k], 0), axis=0, keepdims=True)
        query_lengths = jnp.concatenate([lengths[k]] * cap, axis=0)
        query_live = query_id[:, :1] // SUBGROUP < query_lengths
        usable = same_image & (key_id // SUBGROUP < key_lengths) & query_live
        query_share = jnp.concatenate([inverse_lengths[k]] * cap, axis=0)
        group_rows = slice(k * rows, (k + 1) * rows)
        picked = []
        for h in range(HEADS):
            low = h * HEAD_DIM // 128 * 128
            high = min(-(-(h + 1) * HEAD_DIM // 128) * 128, inner)
            window = (column_id[:, low:high] >= h * HEAD_DIM) & (column_id[:, low:high] < (h + 1) * HEAD_DIM)
            queries = packed_ref[0, group_rows, low:high] * window.astype(jnp.bfloat16)
            keys = packed_ref[1, group_rows, low:high]
            scores = lax.dot_general(queries, keys, NT, preferred_element_type=jnp.float32) * HEAD_DIM ** (-0.5)
            raised = jnp.where(usable, jnp.minimum(jnp.exp(scores), largest), 0.0).astype(jnp.bfloat16)
            denominators = jnp.dot(raised, ones, preferred_element_type=jnp.float32)
            share = jnp.where(query_live, query_share / denominators, 0.0)
            share = jnp.concatenate([share, share[:, : rows - 128]], axis=1)
            weights = raised.astype(jnp.float32) * share
            picked.append(jnp.sum(weights.reshape(cap, SUBGROUP, rows), axis=0))
        stacked = jnp.concatenate(picked, axis=0).astype(jnp.bfloat16)
        mixed = jnp.dot(stacked, packed_ref[2, group_rows, :], preferred_element_type=jnp.float32)
        return jnp.sum(mixed.reshape(HEADS, SUBGROUP, inner) * head_mask, axis=0)

    for members in (range(groups - 1), range(groups - 1, groups)):
        for k in members:
            pool_ref[k * SUBGROUP : (k + 1) * SUBGROUP, :] = pool_group(k)
        span = slice(members[0] * SUBGROUP, (members[-1] + 1) * SUBGROUP)
        result = mean_ref[span, :] + split_dot(pool_ref[span, :], wo_ref[...])
        wide_ref[span, 0, :] = result[:, :half]
        filler = jnp.zeros((result.shape[0], 2 * half - width), jnp.float32)
        wide_ref[span, 1, :] = jnp.concatenate([result[:, half:], filler], axis=1)
        for k in members:
            base = order[k] * SUBGROUP
            sent_ref[pl.ds(base, SUBGROUP)] = wide_ref[k * SUBGROUP : (k + 1) * SUBGROUP].astype(jnp.bfloat16)

            def send(step, carry, base=base):
                to = base + lax.rem(me + step, SUBGROUP)
                pltpu.make_async_remote_copy(
                    sent_ref.at[to], arrived_ref.at[me], send_sem, recv_sem, device_id={"dp": to}, device_id_type=MESH
                ).start()
                return carry

            lax.fori_loop(1 if k == groups - 1 else 0, SUBGROUP, send, 0)
    arrived_ref[me] = sent_ref[me]

    def take_text(k):
        text_copies[k].wait_recv()
        label_copies[k].wait_recv()

    take_text(2)
    pass_text(6, left, right)
    take_text(1)
    pass_text(7, across(right), left)
    pass_text(8, left, sibling)
    pass_text(9, across(right), sibling)
    for k in (4, 3, 0):
        take_text(k)
        pass_text({4: 10, 3: 11, 0: 12}[k], sources[k], sibling)

    lane = lax.broadcasted_iota(jnp.int32, (dests, dests), 1)
    sublane = lax.broadcasted_iota(jnp.int32, (dests, dests), 0)
    intake = jnp.sum(jnp.where(lane == me, counts_ref[...], 0), axis=1, keepdims=True)
    living = (intake > 0).astype(jnp.int32)
    living_row = row_of(living)
    ranking_row = jnp.sum(jnp.where(sublane < lane, living, 0), axis=0, keepdims=True)
    image_id = lax.broadcasted_iota(jnp.int32, (images, dests), 0)
    chooser = ((ranking_row == image_id) & (living_row > 0)).astype(jnp.bfloat16)

    batch = 4
    wide = batch * images

    take_text(6)
    pass_text(13, opposite, sibling)
    take_text(7)
    pass_text(14, across(opposite), sibling)

    pltpu.make_async_remote_copy(
        sent_ref.at[pl.ds(0, dests - 1)], arrived_ref.at[pl.ds(0, dests - 1)], send_sem, recv_sem,
        device_id={"dp": lax.rem(me + 1, dests)}, device_id_type=MESH,
    ).wait()
    wide_ref[...] = arrived_ref[...].astype(jnp.float32)
    for low, high, lane_half in ((0, half, 0), (half, width, 1)):
        values = wide_ref[:, lane_half, : high - low].astype(jnp.bfloat16)
        chosen = jnp.dot(chooser, values, preferred_element_type=jnp.float32)
        img_ref[:, low:high] = chosen.astype(img_ref.dtype)

    gathered_ref[place] = img_ref[...]

    pieces = images // PIECE
    started = []

    def put(stage, c, block, to):
        span = pl.ds(c * PIECE, PIECE)
        spot = gathered_ref.at[block, span]
        k = stage * pieces + c
        copy = pltpu.make_async_remote_copy(
            img_ref.at[span] if block is place else spot, spot, send_sems.at[k], recv_sems.at[k],
            device_id={"blk": to}, device_id_type=MESH,
        )
        copy.start()
        started.append(copy)
        return copy

    own = img_ref[...]
    own_scale = inverse_norms(own.astype(jnp.float32))
    text = text_ref[...]
    text_scale = inverse_norms(text.astype(jnp.float32))
    label_column = column_of(label_ref[...])
    lane_id = lax.broadcasted_iota(jnp.int32, (images, wide), 1)
    text_id = place * images + lax.broadcasted_iota(jnp.int32, (images, wide), 0)

    def image_batch(q):
        others = texts_ref[batch * q : batch * (q + 1)].reshape(wide, width)
        matching = label_column == lane_id + q * wide
        margins, weights = pair_terms(own, own_scale, others, matching)
        losses = jnp.maximum(margins, 0.0) + jnp.log1p(jnp.exp(-jnp.abs(margins)))
        gradient = split_dot(weights, others)
        if q == 0:
            img_grad_ref[...] = gradient
            return losses
        img_grad_ref[...] += gradient
        return losses

    def text_batch(head, is_first):
        first = lax.div(head, batch) * batch
        others = gathered_ref[pl.ds(first, batch)].reshape(wide, width)
        labels = [labels_ref[first + i, 0:1, :images] for i in range(batch)]
        matching = jnp.concatenate(labels, axis=1) == text_id
        _, weights = pair_terms(text, text_scale, others, matching)
        gradient = split_dot(weights, others)
        if is_first:
            text_grad_ref[...] = gradient
        else:
            text_grad_ref[...] += gradient

    each = range(pieces)
    to_right = [put(0, c, place, right) for c in each]
    to_left = [put(1, c, place, left) for c in each]
    to_beside = [put(2, c, place, beside) for c in each]
    to_sibling = [put(3, c, place, sibling) for c in each]
    sibling_waits = []
    beside_right, beside_left, opposite_own = [], [], []
    for c in each:
        to_beside[c].wait_recv()
        beside_right.append(put(4, c, beside, right))
        beside_left.append(put(5, c, beside, left))
        to_right[c].wait_recv()
        to_left[c].wait_recv()
        opposite_own.append(put(6, c, right, left) if c == 1 else put(6, c, left, right))
        sibling_waits.append(put(7, c, beside, sibling))
        sibling_waits.append(put(8, c, left, sibling))
        sibling_waits.append(put(9, c, right, sibling))

    for k in (5, 8, 9, 10, 11, 12, 13, 14):
        take_text(k)
    losses = image_batch(0)
    opposite_beside = []
    for c in each:
        beside_right[c].wait_recv()
        beside_left[c].wait_recv()
        opposite_beside.append(put(10, c, across(left), right) if c == 1 else put(10, c, across(right), left))
        sibling_waits.append(put(11, c, across(left), sibling))
        sibling_waits.append(put(12, c, across(right), sibling))
        if c + 1 < blocks // batch:
            losses = losses + image_batch(c + 1)
    for q in range(pieces + 1, blocks // batch):
        losses = losses + image_batch(q)

    for copy in to_sibling:
        copy.wait_recv()
    for copy in sibling_waits[0::3][:pieces]:
        copy.wait_recv()
    text_batch(place, True)
    for c in each:
        opposite_own[c].wait_recv()
        last_own = put(13, c, opposite, sibling)
        opposite_beside[c].wait_recv()
        last_beside = put(14, c, across(opposite), sibling)
        started_last = (last_own, last_beside)
        sibling_waits.extend(started_last)
    for copy in sibling_waits[1 : 3 * pieces : 3] + sibling_waits[2 : 3 * pieces : 3]:
        copy.wait_recv()
    for copy in sibling_waits[3 * pieces : 5 * pieces]:
        copy.wait_recv()
    text_batch(left, False)
    text_batch(right, False)
    loss_ref[...] = row_of(jnp.sum(losses, axis=1, keepdims=True))
    for copy in sibling_waits[5 * pieces :]:
        copy.wait_recv()
    text_batch(opposite, False)
    for copy in started + text_copies + label_copies:
        copy.wait_send()


def main_call(patch_rows, count_table, w_qkv_t, w_out, own_texts, labels, blocks):
    cap, dests, width = patch_rows.shape
    images = own_texts.shape[0]
    inner = HEADS * HEAD_DIM
    half = -(-width // 256) * 128
    copies = 15 * (images // PIECE)
    vmem = pl.BlockSpec(memory_space=pltpu.VMEM)
    hbm = pl.BlockSpec(memory_space=pl.ANY)
    dma = pltpu.SemaphoreType.DMA
    return pl.pallas_call(
        main_kernel,
        out_shape=(
            jax.ShapeDtypeStruct((images, width), jnp.bfloat16),
            jax.ShapeDtypeStruct((1, images), jnp.float32),
            jax.ShapeDtypeStruct((images, width), jnp.float32),
            jax.ShapeDtypeStruct((images, width), jnp.float32),
        ),
        in_specs=[hbm, vmem, hbm, hbm, vmem, vmem],
        out_specs=(vmem,) * 4,
        scratch_shapes=[
            pltpu.VMEM((cap, dests, width), jnp.bfloat16),
            pltpu.VMEM(w_qkv_t.shape, jnp.bfloat16),
            pltpu.VMEM(w_out.shape, jnp.bfloat16),
            pltpu.VMEM((cap * dests, width), jnp.bfloat16),
            pltpu.VMEM((3, cap * dests, inner), jnp.bfloat16),
            pltpu.VMEM((dests, width), jnp.float32),
            pltpu.VMEM((dests, inner), jnp.float32),
            pltpu.VMEM((dests, 2, half), jnp.float32),
            pltpu.VMEM((dests, 2, half), jnp.bfloat16),
            pltpu.VMEM((dests, 2, half), jnp.bfloat16),
            pltpu.VMEM((blocks, images, width), jnp.bfloat16),
            pltpu.VMEM((blocks, 8, 128), jnp.int32),
            pltpu.VMEM((blocks, images, width), jnp.bfloat16),
            dma((5,)),
            dma,
            dma,
            dma((30,)),
            dma((30,)),
            dma((copies,)),
            dma((copies,)),
        ],
        compiler_params=pltpu.CompilerParams(
            collective_id=0, has_side_effects=True, vmem_limit_bytes=56 * 2**20
        ),
        cost_estimate=pl.CostEstimate(flops=6 * 10**9, bytes_accessed=8 * 10**6, transcendentals=10**6),
        name="main",
    )(patch_rows, count_table, w_qkv_t, w_out, own_texts, labels)


def finish_kernel(img_ref, img_grad_ref, text_ref, text_grad_ref, loss_ref, d_img_ref, d_text_ref, losses_ref):
    for rows_ref, grad_ref, out_ref in ((img_ref, img_grad_ref, d_img_ref), (text_ref, text_grad_ref, d_text_ref)):
        rows = rows_ref[...]
        out_ref[...] = tangent(rows, inverse_norms(rows.astype(jnp.float32)), logit_scale * grad_ref[...])
    losses_ref[...] = loss_ref[...]


def finish(img, img_grad, text, text_grad, losses):
    vmem = pl.BlockSpec(memory_space=pltpu.VMEM)
    return pl.pallas_call(
        finish_kernel,
        out_shape=tuple(jax.ShapeDtypeStruct(v.shape, jnp.float32) for v in (img, text, losses)),
        in_specs=[vmem] * 5,
        out_specs=(vmem,) * 3,
        name="finish",
    )(img, img_grad, text, text_grad, losses)


def local(patches, counts, w_qkv, w_out, text_rows, labels):
    own_texts = text_rows[0]
    patch_rows = jnp.transpose(patches[0, 0], (1, 0, 2))
    img, losses, img_grad, text_grad = main_call(
        patch_rows, counts[0], w_qkv.T, w_out, own_texts, labels, lax.axis_size("blk")
    )
    d_pooled, d_texts, losses = finish(img, img_grad, own_texts, text_grad, losses)
    return (losses, d_pooled[None], d_texts[None])


def solution(mesh):
    in_specs = (
        P("blk", "dp", None, None, None),
        P("blk", None, None),
        P(),
        P(),
        P("dp", "blk", None),
        P("dp", "blk"),
    )
    out_specs = (P("dp", "blk"), P("dp", "blk", None), P("dp", "blk", None))
    return jax.shard_map(local, mesh=mesh, in_specs=in_specs, out_specs=out_specs, check_vma=False)
```
